512 devices in a mesh: wide: 64 (over z, y), narrow: 8 (over x, core).
Axes of the slice: x: 4, y: 8, z: 8, core: 2. Of those that a mesh axis runs over, the one named last changes fastest.
Arguments:
- matrix: bfloat16 [16384, 16384], P('wide', 'narrow'), may hold values from 0.002 to 18
- in_rows: int32 [64, 4], replicated, may hold values from 0 to 63, all different within a row; in each aligned block of 8 rows (0 to 7, 8 to 15, ...) no two rows name the same one
- keep: int32 [64, 4, 2], replicated, may hold values 0 or 1
Outputs:
- clustered: bfloat16 [16384, 16384], P('wide', 'narrow')
The draws below stay inside these ranges and needn't reach their ends.
Inputs may be any that keep to these rules, and one draw needn't show every extreme that they name: `in_rows`: each row names 4 different tile rows. In each aligned block of 8 rows (the tile columns of one index of narrow) no tile row is named by more than 1 row, and some tile row is named by exactly 1.
All inputs are finite; a program needn't handle non-finite values.
Results may differ from the reference program's by a relative error of at most 0.001.
Values may be sent and summed in bfloat16 or wider, within the bound.
A program may use at most 128 MiB of HBM per device.

```python
import math
from functools import partial
import jax
import jax.numpy as jnp
import numpy as np
from jax import lax

TILE = 256
KIN = 4
KEEP = 2
NT = 64
CB = 8
CAP = 1


def draw_matrix(key, part):
    key = jax.random.fold_in(key, 11)
    label_key, row_key, col_key, base_key = jax.random.split(key, 4)
    extent = NT * TILE
    labels = jax.random.randint(label_key, (extent,), 0, 16)
    row_level = jax.random.uniform(row_key, (extent,), jnp.float32, -1.15, 1.15)
    col_level = jax.random.uniform(col_key, (extent,), jnp.float32, -0.55, 0.55)
    lowest = 0.05
    boost = 8.0
    base = jax.random.uniform(base_key, (extent, extent), jnp.float32, lowest, 1.0)
    same = labels[:, None] == labels[None, :]
    factor = jnp.where(same, jnp.float32(1.0 + boost), jnp.float32(1.0))
    return (0.25 * base * factor * jnp.exp(row_level[:, None] + col_level[None, :])).astype(jnp.bfloat16)


def plant(values, key, least, high):
    longest = values.shape.index(max(values.shape))
    spots = []
    for shift in (0, 1):
        where = [jax.random.randint(jax.random.fold_in(key, axis), (), 0, length) for axis, length in enumerate(values.shape)]
        where[longest] = (where[longest] + shift) % values.shape[longest]
        spots.append(tuple(where))
    return values.at[spots[0]].set(least).at[spots[1]].set(high)


def shared_out(stream_key, own, number, rows, count, top, bound, skew):
    sequence = jax.random.permutation(stream_key, count)
    heavy_load, ordinary = portions_of(count, rows * top, bound, skew, True), portions_of(count, rows * top, bound, skew, False)
    places = jnp.arange(count)

    def named(tallies, offset_by):
        used = int((tallies > 0).sum())
        fixed = max(1, used // 4)
        passed = fixed + (places - fixed + offset_by * (used - fixed)) % max(1, count - fixed)
        return jnp.zeros((count,), jnp.int32).at[sequence[jnp.where(places < fixed, places, passed)]].set(jnp.asarray(tallies, jnp.int32))

    tallies = jnp.where(number % 4 == 0, named(heavy_load, number // 4), named(ordinary, number - number // 4 - 1))
    mixed = jax.random.permutation(jax.random.fold_in(own, 3), count)
    donor, taker = mixed[0:count // 2 * 2:2], mixed[1:count // 2 * 2:2]
    margin = jnp.minimum(tallies[donor] - 1, bound - tallies[taker]) // 2
    margin = jnp.where((donor == sequence[0]) | (taker == sequence[0]) | (tallies[taker] == 0), 0, jnp.maximum(margin, 0))
    passed = jax.random.randint(jax.random.fold_in(own, 4), (count // 2,), 0, 1 << 20) % (margin + 1)
    tallies = tallies.at[donor].add(-passed).at[taker].add(passed)
    members = jnp.searchsorted(jnp.cumsum(tallies), jnp.arange(rows * top), side="right").astype(jnp.int32)
    grid = members.reshape(top, rows).T
    grid = grid[jax.random.permutation(jax.random.fold_in(own, 1), rows)]
    offset_by = jax.random.randint(jax.random.fold_in(own, 2), (rows, 1), 0, top)
    return jnp.take_along_axis(grid, (jnp.arange(top)[None, :] + offset_by) % top, axis=1)


def portions_of(count, total, most, slope, full):
    weights = [(1 << 20) // math.isqrt(standing ** slope) + 1 for standing in range(1, count + 1)]
    largest = most if full else min(most, max(-(-total // count), total * weights[0] // sum(weights)))
    least = 1 if total - largest >= count - 1 else 0
    given, spare = [largest] + [least] * (count - 1), total - largest - least * (count - 1)
    while spare > 0:
        free = [i for i in range(1, count) if given[i] < largest] or [i for i in range(1, count) if given[i] < most]
        mass, remaining = sum([weights[i] for i in free]), spare
        for i in free:
            extra = min(most - given[i], max(1, remaining * weights[i] // mass), spare)
            given[i] = given[i] + extra
            spare = spare - extra
    return np.array(given)


def setup_inputs(seed: int = 0) -> dict:
    key_list = jax.random.split(jax.random.key(seed), 4)
    matrix = draw_matrix(jax.random.fold_in(key_list[3], 71), 0)
    in_rows_keys = jax.random.split(jax.random.fold_in(key_list[1], 1), NT // CB)
    in_rows_turns = jax.random.permutation(jax.random.fold_in(key_list[1], 3), NT // CB)
    in_rows = jax.vmap(lambda own, number: shared_out(jax.random.fold_in(key_list[1], 2), own, number, CB, NT, KIN, CAP, 2))(in_rows_keys, in_rows_turns).reshape((NT, KIN))
    keep = plant((jax.random.randint(key_list[2], (NT, KIN, KEEP), 0, 2) < 1).astype(jnp.int32), jax.random.fold_in(key_list[2], 1), 0, 1)
    return {"matrix": matrix, "in_rows": in_rows, "keep": keep}


def one_column(tiles, in_rows, keep, column):
    inner_rows = in_rows[column]
    b_tiles = tiles[inner_rows, :, column, :]
    row_sets = in_rows[inner_rows]
    a_tiles = tiles[row_sets, :, inner_rows[:, None], :]
    products = jnp.einsum("stij,sjl->stil", a_tiles.astype(jnp.float32), b_tiles.astype(jnp.float32), precision=lax.Precision.HIGHEST)
    gathered = jnp.zeros((NT, TILE, TILE), jnp.float32).at[row_sets.reshape(-1)].add(products.reshape(-1, TILE, TILE))
    forced = (jnp.arange(KIN, dtype=jnp.int32)[:, None] == 0) & (jnp.arange(KEEP, dtype=jnp.int32)[None, :] == 0)
    chosen = (keep[column] == 1) | forced
    candidates = row_sets[:, :KEEP]
    kept_rows = jnp.any((candidates[:, :, None] == jnp.arange(NT, dtype=jnp.int32)[None, None, :]) & chosen[:, :, None], axis=(0, 1))
    pruned = jnp.where(kept_rows[:, None, None], gathered, jnp.float32(0.0))
    inflated = pruned * pruned
    totals = jnp.sum(inflated, axis=(0, 1))
    return (TILE * inflated / totals[None, None, :]).astype(jnp.bfloat16)


def reference(matrix, in_rows, keep):
    tiles = matrix.reshape(NT, TILE, NT, TILE)
    columns = lax.map(partial(one_column, tiles, in_rows, keep), jnp.arange(NT, dtype=jnp.int32))
    return jnp.transpose(columns, (1, 2, 0, 3)).reshape(NT * TILE, NT * TILE)
```

```python
import jax
import jax.numpy as jnp
from jax import lax
from jax.experimental import pallas as pl
from jax.experimental.pallas import tpu as pltpu
from jax.sharding import PartitionSpec as P

TILE = 256
RING = 8
COLS = 8
FAN = 4
KEEP = 2
CHUNKS = 2
HEIGHT = TILE // CHUNKS
MESH = pl.DeviceIdType.MESH


def kernel(
    in_rows,
    keep,
    matrix,
    out,
    cols,
    outgoing,
    slots,
    panel,
    infl,
    sums,
    result,
    load_sem,
    store_sem,
    y_send,
    y_recv,
    z_send,
    z_recv,
    x_send,
    x_recv,
    t_send,
    t_recv,
    *rings,
):
    row = lax.axis_index("wide")
    block = lax.axis_index("narrow")
    z = row // RING
    y = row % RING

    def along_y(step):
        return {"wide": z * RING + (y + step + RING) % RING}

    def along_z(step):
        return {"wide": ((z + step + RING) % RING) * RING + y}

    def along_x(step):
        return {"narrow": (block + step) % COLS}

    barrier = pltpu.get_barrier_semaphore()
    for step in range(1, RING):
        for target in (along_y(step), along_z(step), along_x(step)):
            pl.semaphore_signal(barrier, inc=1, device_id=target, device_id_type=MESH)
    loads = []
    for col in range(COLS):
        load = pltpu.make_async_copy(
            matrix.at[:, pl.ds(col * TILE, TILE)], cols.at[col], load_sem.at[col]
        )
        load.start()
        loads.append(load)

    mine = jnp.int32(0)
    for col in range(COLS):
        for s in range(FAN):
            mine = jnp.where(in_rows[block * COLS + col, s] == row, col, mine)
    holder = [jnp.int32(0) for _ in range(RING)]
    for k in range(RING):
        for t in range(FAN):
            named = in_rows[z * RING + k, t]
            for d in range(RING):
                hit = named == ((z + d) % RING) * RING + y
                holder[d] = jnp.where(hit, (k - y + RING) % RING, holder[d])

    for load in loads:
        load.wait()
    slots[RING] = jnp.zeros((TILE, TILE), jnp.bfloat16)
    own = cols[mine]
    for chunk, ring in enumerate(rings):
        ring[0] = own[chunk * HEIGHT : (chunk + 1) * HEIGHT]
    panel[0] = own
    pl.semaphore_wait(barrier, 3 * (RING - 1))

    started = []

    def send(src, dst, send_sem, recv_sem, target):
        copy = pltpu.make_async_remote_copy(
            src_ref=src,
            dst_ref=dst,
            send_sem=send_sem,
            recv_sem=recv_sem,
            device_id=target,
            device_id_type=MESH,
        )
        copy.start()
        started.append(copy)
        return copy

    half = HEIGHT // 2
    moves = {}

    def ring_step(chunk, step):
        ring = rings[chunk]
        up = pl.ds(0, HEIGHT if step < 4 else half)
        down = pl.ds(0, HEIGHT) if step < 4 else pl.ds(half, half)
        if step > 1:
            for copy in moves[chunk, step - 1]:
                copy.wait_recv()
        moves[chunk, step] = (
            send(
                ring.at[(1 - step) % RING, up],
                ring.at[-step % RING, up],
                y_send.at[chunk, 0, step - 1],
                y_recv.at[chunk, 0, step - 1],
                along_y(1),
            ),
            send(
                ring.at[step - 1, down],
                ring.at[step, down],
                y_send.at[chunk, 1, step - 1],
                y_recv.at[chunk, 1, step - 1],
                along_y(-1),
            ),
        )

    across = []

    def hand_out(chunk):
        for copy in moves[chunk, 4]:
            copy.wait_recv()
        ring = rings[chunk]
        rows = pl.ds(chunk * HEIGHT, HEIGHT)
        for d in (4, 3, 5, 2, 6, 1, 7):
            outgoing[d, rows] = ring[holder[d]]
            across.append(
                send(
                    outgoing.at[d, rows],
                    slots.at[-d % RING, rows],
                    z_send.at[chunk, d - 1],
                    z_recv.at[chunk, d - 1],
                    along_z(d),
                )
            )
        slots[0, rows] = ring[holder[0]]

    for wave in range(CHUNKS + 5):
        for chunk in range(CHUNKS):
            step = wave - chunk
            if 1 <= step <= 4:
                ring_step(chunk, step)
            if step == 5:
                hand_out(chunk)
        if wave == 1:
            gathers = [
                send(
                    panel.at[0],
                    panel.at[-d % COLS],
                    x_send.at[d - 1],
                    x_recv.at[d - 1],
                    along_x(d),
                )
                for d in (4, 3, 5, 2, 6, 1, 7)
            ]

    lefts, rights, kept = [], [], []
    for col in range(COLS):
        column = block * COLS + col
        is_kept = jnp.bool_(False)
        for s in range(FAN):
            inner = in_rows[column, s]
            meets = jnp.bool_(False)
            for t in range(FAN):
                names = in_rows[inner, t] == row
                meets = meets | names
                if t < KEEP:
                    if s == 0 and t == 0:
                        is_kept = is_kept | names
                    else:
                        is_kept = is_kept | (names & (keep[column, s, t] == 1))
            group = inner // RING
            lefts.append((group - block + COLS) % COLS)
            rights.append(jnp.where(meets, (group - z + RING) % RING, RING))
        kept.append(is_kept)

    for copy in gathers:
        copy.wait_recv()
    for copy in across:
        copy.wait_recv()

    for col in range(COLS):
        total = jnp.zeros((TILE, TILE), jnp.float32)
        for s in range(FAN):
            i = col * FAN + s
            total += jnp.dot(
                panel[lefts[i]], slots[rights[i]], preferred_element_type=jnp.float32
            )
        total = jnp.where(kept[col], total, jnp.float32(0.0))
        square = total * total
        infl[col] = square
        sums[0, pl.ds(col, 1)] = jnp.sum(square, axis=0, keepdims=True)

    def add_up(first, move):
        copies = [
            send(
                sums.at[first],
                sums.at[first + d],
                t_send.at[first + d - 1],
                t_recv.at[first + d - 1],
                move(d),
            )
            for d in range(1, RING)
        ]
        for copy in copies:
            copy.wait_recv()
        total = sums[first]
        for d in range(1, RING):
            total += sums[first + d]
        return total

    sums[RING] = add_up(0, along_y)
    scale = jnp.float32(TILE) / add_up(RING, along_z)

    stores = []
    for col in range(COLS):
        result[col] = (infl[col] * scale[col : col + 1]).astype(jnp.bfloat16)
        store = pltpu.make_async_copy(
            result.at[col], out.at[:, pl.ds(col * TILE, TILE)], store_sem.at[col]
        )
        store.start()
        stores.append(store)
    for copy in started:
        copy.wait_send()
    for store in stores:
        store.wait()


def on_device(matrix, in_rows, keep):
    tile = (TILE, TILE)
    dma = pltpu.SemaphoreType.DMA
    return pl.pallas_call(
        kernel,
        out_shape=jax.ShapeDtypeStruct(matrix.shape, jnp.bfloat16),
        in_specs=[
            pl.BlockSpec(memory_space=pltpu.SMEM),
            pl.BlockSpec(memory_space=pltpu.SMEM),
            pl.BlockSpec(memory_space=pl.ANY),
        ],
        out_specs=pl.BlockSpec(memory_space=pl.ANY),
        scratch_shapes=[
            pltpu.VMEM((COLS, *tile), jnp.bfloat16),
            pltpu.VMEM((RING, *tile), jnp.bfloat16),
            pltpu.VMEM((RING + 1, *tile), jnp.bfloat16),
            pltpu.VMEM((COLS, *tile), jnp.bfloat16),
            pltpu.VMEM((COLS, *tile), jnp.float32),
            pltpu.VMEM((2 * RING, COLS, TILE), jnp.float32),
            pltpu.VMEM((COLS, *tile), jnp.bfloat16),
            dma((COLS,)),
            dma((COLS,)),
            dma((CHUNKS, 2, 4)),
            dma((CHUNKS, 2, 4)),
            dma((CHUNKS, RING - 1)),
            dma((CHUNKS, RING - 1)),
            dma((COLS - 1,)),
            dma((COLS - 1,)),
            dma((2 * RING - 1,)),
            dma((2 * RING - 1,)),
            *[pltpu.VMEM((RING, HEIGHT, TILE), jnp.bfloat16)] * CHUNKS,
        ],
        compiler_params=pltpu.CompilerParams(
            collective_id=0, has_side_effects=True, vmem_limit_bytes=40 << 20
        ),
    )(in_rows, keep, matrix)


def solution(mesh):
    return jax.shard_map(
        on_device,
        mesh=mesh,
        in_specs=(P("wide", "narrow"), P(), P()),
        out_specs=P("wide", "narrow"),
        check_vma=False,
    )
```

```python
import jax
import jax.numpy as jnp
from jax import lax
from jax.experimental import pallas as pl
from jax.experimental.pallas import tpu as pltpu
from jax.sharding import PartitionSpec as P

TILE = 256
RING = 8
COLS = 8
FAN = 4
KEEP = 2
UPPER = 128
HEIGHT = 64
PIECE = 16
FAR_FIRST = (4, 3, 5, 2, 6, 1, 7)
MESH = pl.DeviceIdType.MESH


def place(step):
    step %= RING
    return 0 if step == 0 else 2 * step - 1 if step <= 4 else 2 * (RING - step)


def kernel(
    in_rows_hbm,
    keep_hbm,
    matrix,
    out,
    in_rows,
    keep,
    cols,
    lower,
    outgoing,
    pieces,
    slots,
    panel,
    infl,
    result,
    sums,
    index_sem,
    load_sem,
    p_send,
    p_recv,
    a_send,
    a_recv,
    r_send,
    r_recv,
    z_send,
    z_recv,
    s_send,
    s_recv,
    x_send,
    x_recv,
    t_send,
    t_recv,
    *bundles,
):
    rings, planes = bundles[:2], bundles[2:]
    row = lax.axis_index("wide")
    block = lax.axis_index("narrow")
    z = row // RING
    y = row % RING

    def along_y(step):
        return {"wide": z * RING + (y + step + RING) % RING}

    def along_z(step):
        return {"wide": ((z + step + RING) % RING) * RING + y}

    def along_x(step):
        return {"narrow": (block + step) % COLS}

    barrier = pltpu.get_barrier_semaphore()
    for step in range(1, RING):
        for target in (along_y(step), along_z(step), along_x(step)):
            pl.semaphore_signal(barrier, inc=1, device_id=target, device_id_type=MESH)
    indices = [
        pltpu.make_async_copy(in_rows_hbm, in_rows, index_sem.at[0]),
        pltpu.make_async_copy(keep_hbm, keep, index_sem.at[1]),
    ]
    for load in indices:
        load.start()
    loads = []
    for col in range(COLS):
        load = pltpu.make_async_copy(
            matrix.at[:, pl.ds(col * TILE, TILE)], cols.at[col], load_sem.at[col]
        )
        load.start()
        loads.append(load)
    for load in indices:
        load.wait()

    mine = jnp.int32(0)
    for col in range(COLS):
        for s in range(FAN):
            mine = jnp.where(in_rows[s, block * COLS + col] == row, col, mine)
    for load in loads:
        load.wait()
    own = cols[mine]
    panel[0] = own
    for chunk in range(2):
        rings[chunk][0] = own[chunk * HEIGHT : (chunk + 1) * HEIGHT]
    lower[...] = own[UPPER:].reshape(RING, PIECE, TILE)
    planes[0][0] = lower[y]
    pl.semaphore_wait(barrier, 3 * (RING - 1))

    started = []

    def send(src, dst, send_sem, recv_sem, target):
        copy = pltpu.make_async_remote_copy(
            src_ref=src,
            dst_ref=dst,
            send_sem=send_sem,
            recv_sem=recv_sem,
            device_id=target,
            device_id_type=MESH,
        )
        copy.start()
        started.append(copy)
        return copy

    def arrive(copies):
        for copy in copies:
            copy.wait_recv()

    parted = [
        send(
            lower.at[(y + d) % RING],
            planes[0].at[-d % RING],
            p_send.at[d - 1],
            p_recv.at[d - 1],
            along_y(d),
        )
        for d in FAR_FIRST
    ]
    spread = [
        [
            send(
                ring.at[0],
                ring.at[-d % RING],
                a_send.at[chunk, d - 1],
                a_recv.at[chunk, d - 1],
                along_y(d),
            )
            for d in FAR_FIRST
        ]
        for chunk, ring in enumerate(rings)
    ]

    def pass_on(step, refs, send_sem, recv_sem, move, size):
        first, second = (0, size), (0, size)
        if step == 4:
            first, second = (0, size // 2), (size // 2, size // 2)
        return (
            send(
                refs[(1 - step) % RING].at[pl.ds(*first)],
                refs[-step % RING].at[pl.ds(*first)],
                send_sem.at[0, step - 1],
                recv_sem.at[0, step - 1],
                move(1),
            ),
            send(
                refs[step - 1].at[pl.ds(*second)],
                refs[step].at[pl.ds(*second)],
                send_sem.at[1, step - 1],
                recv_sem.at[1, step - 1],
                move(-1),
            ),
        )

    def z_step(step):
        return pass_on(step, planes, r_send, r_recv, along_z, RING)

    gathers = [
        send(
            panel.at[0],
            panel.at[-d % COLS],
            x_send.at[d - 1],
            x_recv.at[d - 1],
            along_x(d),
        )
        for d in FAR_FIRST
    ]

    def holders(group, rows):
        found = [jnp.int32(0) for _ in rows]
        for k in range(RING):
            for t in range(FAN):
                named = in_rows[t, group * RING + k]
                for i, wanted in enumerate(rows):
                    found[i] = jnp.where(named == wanted, k, found[i])
        return [(k - y + RING) % RING for k in found]

    to_planes = holders(z, [((z + d) % RING) * RING + y for d in range(RING)])
    in_plane = [z * RING + (y + d) % RING for d in range(RING)]
    to_devices = {}
    for g in range(RING):
        to_devices[g] = holders((z + g) % RING, in_plane)

    across = []

    def hand_out(chunk):
        rows = pl.ds(chunk * HEIGHT, HEIGHT)
        for d in FAR_FIRST:
            outgoing[d, rows] = rings[chunk][to_planes[d]]
            across.append(
                send(
                    outgoing.at[d, rows],
                    slots.at[place(-d), rows],
                    z_send.at[chunk, d - 1],
                    z_recv.at[chunk, d - 1],
                    along_z(d),
                )
            )
        slots[0, rows] = rings[chunk][to_planes[0]]

    here = pl.ds(pl.multiple_of(UPPER + y * PIECE, PIECE), PIECE)

    def deal(distance):
        both = sorted({distance, -distance % RING})
        first = place(distance)
        group = pl.ds(first, len(both))
        for d in FAR_FIRST + (0,):
            for g in both:
                piece = planes[g][to_devices[g][d]]
                if d == 0:
                    slots[place(g), here] = piece
                else:
                    pieces[place(g), d] = piece
            if d:
                across.append(
                    send(
                        pieces.at[group, d],
                        slots.at[group, here],
                        s_send.at[distance, d - 1],
                        s_recv.at[distance, d - 1],
                        along_y(d),
                    )
                )

    arrive(parted)
    z_moves = z_step(1)
    deal(0)
    arrive(z_moves)
    z_moves = z_step(2)
    deal(1)
    arrive(spread[0])
    hand_out(0)
    arrive(z_moves)
    z_moves = z_step(3)
    deal(2)
    arrive(z_moves)
    z_moves = z_step(4)
    deal(3)
    arrive(spread[1])
    hand_out(1)
    arrive(z_moves)
    deal(4)

    slots[RING] = jnp.zeros((TILE, TILE), jnp.bfloat16)
    lefts, rights, kept = [], [], []
    for col in range(COLS):
        column = block * COLS + col
        is_kept = jnp.bool_(False)
        for s in range(FAN):
            inner = in_rows[s, column]
            meets = jnp.bool_(False)
            for t in range(FAN):
                names = in_rows[t, inner] == row
                meets = meets | names
                if t < KEEP:
                    if s == 0 and t == 0:
                        is_kept = is_kept | names
                    else:
                        is_kept = is_kept | (names & (keep[s, t, column] == 1))
            group = inner // RING
            lefts.append((group - block + COLS) % COLS)
            step = (group - z + RING) % RING
            slot = jnp.where(step <= 4, jnp.maximum(2 * step - 1, 0), 2 * (RING - step))
            rights.append(jnp.where(meets, slot, RING))
        kept.append(is_kept)

    arrive(gathers)
    arrive(across)

    for col in range(COLS):
        total = jnp.zeros((TILE, TILE), jnp.float32)
        for s in range(FAN):
            i = col * FAN + s
            total += jnp.dot(
                panel[lefts[i]], slots[rights[i]], preferred_element_type=jnp.float32
            )
        total = jnp.where(kept[col], total, jnp.float32(0.0))
        square = total * total
        infl[col] = square
        sums[0, pl.ds(col, 1)] = jnp.sum(square, axis=0, keepdims=True)

    def add_up(first, move):
        copies = [
            send(
                sums.at[first],
                sums.at[first + d],
                t_send.at[first + d - 1],
                t_recv.at[first + d - 1],
                move(d),
            )
            for d in FAR_FIRST
        ]
        arrive(copies)
        total = sums[first]
        for d in range(1, RING):
            total += sums[first + d]
        return total

    sums[RING] = add_up(0, along_y)
    scale = jnp.float32(TILE) / add_up(RING, along_z)
    stores = []
    for col in range(COLS):
        result[col] = (infl[col] * scale[col : col + 1]).astype(jnp.bfloat16)
        store = pltpu.make_async_copy(
            result.at[col], out.at[:, pl.ds(col * TILE, TILE)], load_sem.at[col]
        )
        store.start()
        stores.append(store)
    for copy in started:
        copy.wait_send()
    for store in stores:
        store.wait()


def on_device(matrix, in_rows, keep):
    tile = (TILE, TILE)
    bundle = (RING, PIECE, TILE)
    dma = pltpu.SemaphoreType.DMA
    others = RING - 1
    hbm = pl.BlockSpec(memory_space=pltpu.HBM)
    return pl.pallas_call(
        kernel,
        out_shape=jax.ShapeDtypeStruct(matrix.shape, jnp.bfloat16),
        in_specs=[hbm, hbm, hbm],
        out_specs=hbm,
        scratch_shapes=[
            pltpu.SMEM((FAN, in_rows.shape[0]), jnp.int32),
            pltpu.SMEM((FAN, KEEP, in_rows.shape[0]), jnp.int32),
            pltpu.VMEM((COLS, *tile), jnp.bfloat16),
            pltpu.VMEM(bundle, jnp.bfloat16),
            pltpu.VMEM((RING, UPPER, TILE), jnp.bfloat16),
            pltpu.VMEM((RING, *bundle), jnp.bfloat16),
            pltpu.VMEM((RING + 1, *tile), jnp.bfloat16),
            pltpu.VMEM((COLS, *tile), jnp.bfloat16),
            pltpu.VMEM((COLS, *tile), jnp.float32),
            pltpu.VMEM((COLS, *tile), jnp.bfloat16),
            pltpu.VMEM((2 * RING, COLS, TILE), jnp.float32),
            dma((2,)),
            dma((COLS,)),
            dma((others,)),
            dma((others,)),
            dma((2, others)),
            dma((2, others)),
            dma((2, 4)),
            dma((2, 4)),
            dma((2, others)),
            dma((2, others)),
            dma((5, others)),
            dma((5, others)),
            dma((others,)),
            dma((others,)),
            dma((2 * RING - 1,)),
            dma((2 * RING - 1,)),
            pltpu.VMEM((RING, HEIGHT, TILE), jnp.bfloat16),
            pltpu.VMEM((RING, HEIGHT, TILE), jnp.bfloat16),
            *[pltpu.VMEM(bundle, jnp.bfloat16)] * RING,
        ],
        compiler_params=pltpu.CompilerParams(
            collective_id=0, has_side_effects=True, vmem_limit_bytes=56 << 20
        ),
    )(in_rows.T, keep.transpose(1, 2, 0), matrix)


def solution(mesh):
    return jax.shard_map(
        on_device,
        mesh=mesh,
        in_specs=(P("wide", "narrow"), P(), P()),
        out_specs=P("wide", "narrow"),
        check_vma=False,
    )
```

```python
import jax
import jax.numpy as jnp
from jax import lax
from jax.experimental import pallas as pl
from jax.experimental.pallas import tpu as pltpu
from jax.sharding import PartitionSpec as P

TILE = 256
RING = 8
COLS = 8
FAN = 4
KEEP = 2
UPPER = 128
HEIGHT = 64
PIECE = 16
FAR_FIRST = (4, 3, 5, 2, 6, 1, 7)
MESH = pl.DeviceIdType.MESH


def place(step):
    step %= RING
    return 0 if step == 0 else 2 * step - 1 if step <= 4 else 2 * (RING - step)


def kernel(
    in_rows_hbm,
    keep_hbm,
    matrix,
    out,
    in_rows,
    keep,
    cols,
    lower,
    outgoing,
    pieces,
    slots,
    panel,
    infl,
    result,
    sums,
    index_sem,
    load_sem,
    p_send,
    p_recv,
    a_send,
    a_recv,
    r_send,
    r_recv,
    z_send,
    z_recv,
    s_send,
    s_recv,
    x_send,
    x_recv,
    t_send,
    t_recv,
    *bundles,
):
    rings, planes = bundles[:2], bundles[2:]
    row = lax.axis_index("wide")
    block = lax.axis_index("narrow")
    z = row // RING
    y = row % RING

    def along_y(step):
        return {"wide": z * RING + (y + step + RING) % RING}

    def along_z(step):
        return {"wide": ((z + step + RING) % RING) * RING + y}

    def along_x(step):
        return {"narrow": (block + step) % COLS}

    barrier = pltpu.get_barrier_semaphore()
    for step in range(1, RING):
        for target in (along_y(step), along_z(step), along_x(step)):
            pl.semaphore_signal(barrier, inc=1, device_id=target, device_id_type=MESH)
    indices = [
        pltpu.make_async_copy(in_rows_hbm, in_rows, index_sem.at[0]),
        pltpu.make_async_copy(keep_hbm, keep, index_sem.at[1]),
    ]
    for load in indices:
        load.start()
    loads = []
    for col in range(COLS):
        load = pltpu.make_async_copy(
            matrix.at[:, pl.ds(col * TILE, TILE)], cols.at[col], load_sem.at[col]
        )
        load.start()
        loads.append(load)
    for load in indices:
        load.wait()

    mine = jnp.int32(0)
    for col in range(COLS):
        for s in range(FAN):
            mine = jnp.where(in_rows[s, block * COLS + col] == row, col, mine)
    for load in loads:
        load.wait()
    own = cols[mine]
    panel[0] = own
    for chunk in range(2):
        rings[chunk][0] = own[chunk * HEIGHT : (chunk + 1) * HEIGHT]
    lower[...] = own[UPPER:].reshape(RING, PIECE, TILE)
    planes[0][0] = lower[y]
    pl.semaphore_wait(barrier, 3 * (RING - 1))

    started = []

    def send(src, dst, send_sem, recv_sem, target):
        copy = pltpu.make_async_remote_copy(
            src_ref=src,
            dst_ref=dst,
            send_sem=send_sem,
            recv_sem=recv_sem,
            device_id=target,
            device_id_type=MESH,
        )
        copy.start()
        started.append(copy)
        return copy

    def arrive(copies):
        for copy in copies:
            copy.wait_recv()

    parted = [
        send(
            lower.at[(y + d) % RING],
            planes[0].at[-d % RING],
            p_send.at[d - 1],
            p_recv.at[d - 1],
            along_y(d),
        )
        for d in FAR_FIRST
    ]
    spread = [
        [
            send(
                ring.at[0],
                ring.at[-d % RING],
                a_send.at[chunk, d - 1],
                a_recv.at[chunk, d - 1],
                along_y(d),
            )
            for d in FAR_FIRST
        ]
        for chunk, ring in enumerate(rings)
    ]

    def z_send_to(source, target, move, i, part=(0, RING)):
        return send(
            planes[source % RING].at[pl.ds(*part)],
            planes[target % RING].at[pl.ds(*part)],
            r_send.at[i],
            r_recv.at[i],
            along_z(move),
        )

    def z_near():
        return [
            z_send_to(0, -2, 2, 0),
            z_send_to(0, 2, -2, 1),
            z_send_to(0, -1, 1, 2),
            z_send_to(0, 1, -1, 3),
        ]

    def z_far_3():
        return [z_send_to(-1, -3, 2, 4), z_send_to(1, 3, -2, 5)]

    def z_far_4():
        half = RING // 2
        return [
            z_send_to(-2, 4, 2, 6, (0, half)),
            z_send_to(2, 4, -2, 7, (half, half)),
        ]

    gathers = [
        send(
            panel.at[0],
            panel.at[-d % COLS],
            x_send.at[d - 1],
            x_recv.at[d - 1],
            along_x(d),
        )
        for d in FAR_FIRST
    ]

    def holders(group, rows):
        found = [jnp.int32(0) for _ in rows]
        for k in range(RING):
            for t in range(FAN):
                named = in_rows[t, group * RING + k]
                for i, wanted in enumerate(rows):
                    found[i] = jnp.where(named == wanted, k, found[i])
        return [(k - y + RING) % RING for k in found]

    to_planes = holders(z, [((z + d) % RING) * RING + y for d in range(RING)])
    in_plane = [z * RING + (y + d) % RING for d in range(RING)]
    to_devices = {}
    for g in range(RING):
        to_devices[g] = holders((z + g) % RING, in_plane)

    across = []

    def hand_out(chunk):
        rows = pl.ds(chunk * HEIGHT, HEIGHT)
        for d in FAR_FIRST:
            outgoing[d, rows] = rings[chunk][to_planes[d]]
            across.append(
                send(
                    outgoing.at[d, rows],
                    slots.at[place(-d), rows],
                    z_send.at[chunk, d - 1],
                    z_recv.at[chunk, d - 1],
                    along_z(d),
                )
            )
        slots[0, rows] = rings[chunk][to_planes[0]]

    here = pl.ds(pl.multiple_of(UPPER + y * PIECE, PIECE), PIECE)

    def deal(distance):
        both = sorted({distance, -distance % RING})
        first = place(distance)
        group = pl.ds(first, len(both))
        for d in FAR_FIRST + (0,):
            for g in both:
                piece = planes[g][to_devices[g][d]]
                if d == 0:
                    slots[place(g), here] = piece
                else:
                    pieces[place(g), d] = piece
            if d:
                across.append(
                    send(
                        pieces.at[group, d],
                        slots.at[group, here],
                        s_send.at[distance, d - 1],
                        s_recv.at[distance, d - 1],
                        along_y(d),
                    )
                )

    arrive(parted)
    near = z_near()
    deal(0)
    arrive(near[2:])
    third = z_far_3()
    arrive(near[:2])
    fourth = z_far_4()
    deal(1)
    deal(2)
    arrive(spread[0])
    hand_out(0)
    arrive(third)
    deal(3)
    arrive(fourth)
    deal(4)
    arrive(spread[1])
    hand_out(1)

    slots[RING] = jnp.zeros((TILE, TILE), jnp.bfloat16)
    lefts, rights, kept = [], [], []
    for col in range(COLS):
        column = block * COLS + col
        is_kept = jnp.bool_(False)
        for s in range(FAN):
            inner = in_rows[s, column]
            meets = jnp.bool_(False)
            for t in range(FAN):
                names = in_rows[t, inner] == row
                meets = meets | names
                if t < KEEP:
                    if s == 0 and t == 0:
                        is_kept = is_kept | names
                    else:
                        is_kept = is_kept | (names & (keep[s, t, column] == 1))
            group = inner // RING
            lefts.append((group - block + COLS) % COLS)
            step = (group - z + RING) % RING
            slot = jnp.where(step <= 4, jnp.maximum(2 * step - 1, 0), 2 * (RING - step))
            rights.append(jnp.where(meets, slot, RING))
        kept.append(is_kept)

    arrive(gathers)
    arrive(across)

    for col in range(COLS):
        total = jnp.zeros((TILE, TILE), jnp.float32)
        for s in range(FAN):
            i = col * FAN + s
            total += jnp.dot(
                panel[lefts[i]], slots[rights[i]], preferred_element_type=jnp.float32
            )
        total = jnp.where(kept[col], total, jnp.float32(0.0))
        square = total * total
        infl[col] = square
        sums[0, pl.ds(col, 1)] = jnp.sum(square, axis=0, keepdims=True)

    def add_up(first, move, earlier):
        copies = [
            send(
                sums.at[first],
                sums.at[first + d],
                t_send.at[first + d - 1],
                t_recv.at[first + d - 1],
                move(d),
            )
            for d in FAR_FIRST
        ]
        for copy in earlier:
            copy.wait_send()
        arrive(copies)
        total = sums[first]
        for d in range(1, RING):
            total += sums[first + d]
        return total

    sums[RING] = add_up(0, along_y, started[:])
    last = started[-(RING - 1) :]
    scale = jnp.float32(TILE) / add_up(RING, along_z, last)
    stores = []
    for col in range(COLS):
        result[col] = (infl[col] * scale[col : col + 1]).astype(jnp.bfloat16)
        store = pltpu.make_async_copy(
            result.at[col], out.at[:, pl.ds(col * TILE, TILE)], load_sem.at[col]
        )
        store.start()
        stores.append(store)
    for copy in started[-(RING - 1) :]:
        copy.wait_send()
    for store in stores:
        store.wait()


def on_device(matrix, in_rows, keep):
    tile = (TILE, TILE)
    bundle = (RING, PIECE, TILE)
    dma = pltpu.SemaphoreType.DMA
    others = RING - 1
    hbm = pl.BlockSpec(memory_space=pltpu.HBM)
    return pl.pallas_call(
        kernel,
        out_shape=jax.ShapeDtypeStruct(matrix.shape, jnp.bfloat16),
        in_specs=[hbm, hbm, hbm],
        out_specs=hbm,
        scratch_shapes=[
            pltpu.SMEM((FAN, in_rows.shape[0]), jnp.int32),
            pltpu.SMEM((FAN, KEEP, in_rows.shape[0]), jnp.int32),
            pltpu.VMEM((COLS, *tile), jnp.bfloat16),
            pltpu.VMEM(bundle, jnp.bfloat16),
            pltpu.VMEM((RING, UPPER, TILE), jnp.bfloat16),
            pltpu.VMEM((RING, *bundle), jnp.bfloat16),
            pltpu.VMEM((RING + 1, *tile), jnp.bfloat16),
            pltpu.VMEM((COLS, *tile), jnp.bfloat16),
            pltpu.VMEM((COLS, *tile), jnp.float32),
            pltpu.VMEM((COLS, *tile), jnp.bfloat16),
            pltpu.VMEM((2 * RING, COLS, TILE), jnp.float32),
            dma((2,)),
            dma((COLS,)),
            dma((others,)),
            dma((others,)),
            dma((2, others)),
            dma((2, others)),
            dma((8,)),
            dma((8,)),
            dma((2, others)),
            dma((2, others)),
            dma((5, others)),
            dma((5, others)),
            dma((others,)),
            dma((others,)),
            dma((2 * RING - 1,)),
            dma((2 * RING - 1,)),
            pltpu.VMEM((RING, HEIGHT, TILE), jnp.bfloat16),
            pltpu.VMEM((RING, HEIGHT, TILE), jnp.bfloat16),
            *[pltpu.VMEM(bundle, jnp.bfloat16)] * RING,
        ],
        compiler_params=pltpu.CompilerParams(
            collective_id=0, has_side_effects=True, vmem_limit_bytes=52 << 20
        ),
    )(in_rows.T, keep.transpose(1, 2, 0), matrix)


def solution(mesh):
    return jax.shard_map(
        on_device,
        mesh=mesh,
        in_specs=(P("wide", "narrow"), P(), P()),
        out_specs=P("wide", "narrow"),
        check_vma=False,
    )
```

```python
import jax
import jax.numpy as jnp
from jax import lax
from jax.experimental import pallas as pl
from jax.experimental.pallas import tpu as pltpu
from jax.sharding import PartitionSpec as P

TILE = 256
RING = 8
COLS = 8
FAN = 4
KEEP = 2
UPPER = 128
CHUNKS = (64, 64)
PIECE = 16
FAR_FIRST = (4, 3, 5, 2, 6, 1, 7)
MESH = pl.DeviceIdType.MESH


def place(step):
    step %= RING
    return 0 if step == 0 else 2 * step - 1 if step <= 4 else 2 * (RING - step)


def kernel(
    index_hbm,
    matrix,
    out,
    in_rows,
    cols,
    lower,
    outgoing,
    pieces,
    slots,
    panel,
    infl,
    result,
    sums,
    index_sem,
    load_sem,
    p_send,
    p_recv,
    y_send,
    y_recv,
    r_send,
    r_recv,
    z_send,
    z_recv,
    s_send,
    s_recv,
    x_send,
    x_recv,
    t_send,
    t_recv,
    *bundles,
):
    rings, planes = bundles[: len(CHUNKS)], bundles[len(CHUNKS) :]
    starts = [sum(CHUNKS[:c]) for c in range(len(CHUNKS))]
    row = lax.axis_index("wide")
    block = lax.axis_index("narrow")
    z = row // RING
    y = row % RING

    def along_y(step):
        return {"wide": z * RING + (y + step + RING) % RING}

    def along_z(step):
        return {"wide": ((z + step + RING) % RING) * RING + y}

    def along_x(step):
        return {"narrow": (block + step) % COLS}

    barrier = pltpu.get_barrier_semaphore()
    for step in range(1, RING):
        for target in (along_y(step), along_z(step), along_x(step)):
            pl.semaphore_signal(barrier, inc=1, device_id=target, device_id_type=MESH)
    index_load = pltpu.make_async_copy(index_hbm, in_rows, index_sem.at[0])
    index_load.start()
    loads = []
    for col in range(COLS):
        load = pltpu.make_async_copy(
            matrix.at[:, pl.ds(col * TILE, TILE)], cols.at[col], load_sem.at[col]
        )
        load.start()
        loads.append(load)
    index_load.wait()

    mine = jnp.int32(0)
    for col in range(COLS):
        for s in range(FAN):
            mine = jnp.where(in_rows[s, block * COLS + col] == row, col, mine)
    for load in loads:
        load.wait()
    own = cols[mine]
    panel[0] = own
    for ring, start, height in zip(rings, starts, CHUNKS):
        ring[0] = own[start : start + height]
    lower[...] = own[UPPER:].reshape(RING, PIECE, TILE)
    planes[0][0] = lower[y]
    pl.semaphore_wait(barrier, 3 * (RING - 1))

    started = []

    def send(src, dst, send_sem, recv_sem, target):
        copy = pltpu.make_async_remote_copy(
            src_ref=src,
            dst_ref=dst,
            send_sem=send_sem,
            recv_sem=recv_sem,
            device_id=target,
            device_id_type=MESH,
        )
        copy.start()
        started.append(copy)
        return copy

    def arrive(copies):
        for copy in copies:
            copy.wait_recv()

    parted = [
        send(
            lower.at[(y + d) % RING],
            planes[0].at[-d % RING],
            p_send.at[d - 1],
            p_recv.at[d - 1],
            along_y(d),
        )
        for d in FAR_FIRST
    ]
    def near(refs, send_sem, recv_sem, move):
        return [
            send(refs[0], refs[-d], send_sem.at[i], recv_sem.at[i], move(d))
            for i, d in enumerate((2, -2, 1, -1))
        ]

    def far(refs, distance, size, send_sem, recv_sem, move):
        copies = []
        for i, way in enumerate((1, -1)):
            part = pl.ds(0, size)
            if distance == 4:
                part = pl.ds(i * (size // 2), size // 2)
            copies.append(
                send(
                    refs[-way * (distance - 2)].at[part],
                    refs[-way * distance].at[part],
                    send_sem.at[2 * distance - 2 + i],
                    recv_sem.at[2 * distance - 2 + i],
                    move(2 * way),
                )
            )
        return copies

    z_sems = r_send, r_recv
    y_sems = [(y_send.at[c], y_recv.at[c]) for c in range(len(CHUNKS))]
    y_refs = [[ring.at[d] for d in range(RING)] for ring in rings]
    y_near = [near(y_refs[c], *y_sems[c], along_y) for c in range(len(CHUNKS))]
    gathers = [
        send(
            panel.at[0],
            panel.at[-d % COLS],
            x_send.at[d - 1],
            x_recv.at[d - 1],
            along_x(d),
        )
        for d in FAR_FIRST
    ]

    def holders(group, rows):
        found = [jnp.int32(0) for _ in rows]
        for k in range(RING):
            for t in range(FAN):
                named = in_rows[t, group * RING + k]
                for i, wanted in enumerate(rows):
                    found[i] = jnp.where(named == wanted, k, found[i])
        return [(k - y + RING) % RING for k in found]

    to_planes = holders(z, [((z + d) % RING) * RING + y for d in range(RING)])
    in_plane = [z * RING + (y + d) % RING for d in range(RING)]
    to_devices = {}
    for g in range(RING):
        to_devices[g] = holders((z + g) % RING, in_plane)

    across = []

    def hand_out(chunk):
        rows = pl.ds(starts[chunk], CHUNKS[chunk])
        for d in FAR_FIRST:
            outgoing[d, rows] = rings[chunk][to_planes[d]]
            across.append(
                send(
                    outgoing.at[d, rows],
                    slots.at[place(-d), rows],
                    z_send.at[chunk, d - 1],
                    z_recv.at[chunk, d - 1],
                    along_z(d),
                )
            )
        slots[0, rows] = rings[chunk][to_planes[0]]

    here = pl.ds(pl.multiple_of(UPPER + y * PIECE, PIECE), PIECE)

    def deal(distance):
        both = sorted({distance, -distance % RING})
        first = place(distance)
        group = pl.ds(first, len(both))
        for d in FAR_FIRST + (0,):
            for g in both:
                piece = planes[g][to_devices[g][d]]
                if d == 0:
                    slots[place(g), here] = piece
                else:
                    pieces[place(g), d] = piece
            if d:
                across.append(
                    send(
                        pieces.at[group, d],
                        slots.at[group, here],
                        s_send.at[distance, d - 1],
                        s_recv.at[distance, d - 1],
                        along_y(d),
                    )
                )

    y_far = {}

    def y_on(chunk):
        arrive(y_near[chunk])
        y_far[chunk] = [
            copy
            for distance in (3, 4)
            for copy in far(y_refs[chunk], distance, CHUNKS[chunk], *y_sems[chunk], along_y)
        ]

    arrive(parted)
    z_near = near(planes, *z_sems, along_z)
    y_on(0)
    arrive(z_near[2:])
    z_third = far(planes, 3, RING, *z_sems, along_z)
    y_on(1)
    arrive(z_near[:2])
    z_fourth = far(planes, 4, RING, *z_sems, along_z)
    deal(0)
    deal(1)
    arrive(y_far[0])
    hand_out(0)
    deal(2)
    arrive(z_third)
    deal(3)
    arrive(y_far[1])
    hand_out(1)
    arrive(z_fourth)
    deal(4)

    slots[RING] = jnp.zeros((TILE, TILE), jnp.bfloat16)
    lefts, rights, kept = [], [], []
    for col in range(COLS):
        column = block * COLS + col
        is_kept = jnp.bool_(False)
        for s in range(FAN):
            inner = in_rows[s, column]
            meets = jnp.bool_(False)
            for t in range(FAN):
                names = in_rows[t, inner] == row
                meets = meets | names
                if t < KEEP:
                    if s == 0 and t == 0:
                        is_kept = is_kept | names
                    else:
                        is_kept = is_kept | (names & (in_rows[FAN + s * KEEP + t, column] == 1))
            group = inner // RING
            lefts.append((group - block + COLS) % COLS)
            step = (group - z + RING) % RING
            slot = jnp.where(step <= 4, jnp.maximum(2 * step - 1, 0), 2 * (RING - step))
            rights.append(jnp.where(meets, slot, RING))
        kept.append(is_kept)

    arrive(gathers)
    arrive(across)

    for col in range(COLS):
        total = jnp.zeros((TILE, TILE), jnp.float32)
        for s in range(FAN):
            i = col * FAN + s
            total += jnp.dot(
                panel[lefts[i]], slots[rights[i]], preferred_element_type=jnp.float32
            )
        total = jnp.where(kept[col], total, jnp.float32(0.0))
        square = total * total
        infl[col] = square
        sums[0, pl.ds(col, 1)] = jnp.sum(square, axis=0, keepdims=True)

    def add_up(first, move, earlier):
        copies = [
            send(
                sums.at[first],
                sums.at[first + d],
                t_send.at[first + d - 1],
                t_recv.at[first + d - 1],
                move(d),
            )
            for d in FAR_FIRST
        ]
        for copy in earlier:
            copy.wait_send()
        arrive(copies)
        total = sums[first]
        for d in range(1, RING):
            total += sums[first + d]
        return total

    sums[RING] = add_up(0, along_y, started[:])
    last = started[-(RING - 1) :]
    scale = jnp.float32(TILE) / add_up(RING, along_z, last)
    stores = []
    for col in range(COLS):
        result[col] = (infl[col] * scale[col : col + 1]).astype(jnp.bfloat16)
        store = pltpu.make_async_copy(
            result.at[col], out.at[:, pl.ds(col * TILE, TILE)], load_sem.at[col]
        )
        store.start()
        stores.append(store)
    for copy in started[-(RING - 1) :]:
        copy.wait_send()
    for store in stores:
        store.wait()


def on_device(matrix, in_rows, keep):
    index = jnp.concatenate([in_rows, keep.reshape(-1, FAN * KEEP)], axis=1).T
    tile = (TILE, TILE)
    bundle = (RING, PIECE, TILE)
    dma = pltpu.SemaphoreType.DMA
    others = RING - 1
    hbm = pl.BlockSpec(memory_space=pltpu.HBM)
    return pl.pallas_call(
        kernel,
        out_shape=jax.ShapeDtypeStruct(matrix.shape, jnp.bfloat16),
        in_specs=[hbm, hbm],
        out_specs=hbm,
        scratch_shapes=[
            pltpu.SMEM(index.shape, jnp.int32),
            pltpu.VMEM((COLS, *tile), jnp.bfloat16),
            pltpu.VMEM(bundle, jnp.bfloat16),
            pltpu.VMEM((RING, UPPER, TILE), jnp.bfloat16),
            pltpu.VMEM((RING, *bundle), jnp.bfloat16),
            pltpu.VMEM((RING + 1, *tile), jnp.bfloat16),
            pltpu.VMEM((COLS, *tile), jnp.bfloat16),
            pltpu.VMEM((COLS, *tile), jnp.float32),
            pltpu.VMEM((COLS, *tile), jnp.bfloat16),
            pltpu.VMEM((2 * RING, COLS, TILE), jnp.float32),
            dma((1,)),
            dma((COLS,)),
            dma((others,)),
            dma((others,)),
            dma((len(CHUNKS), 8)),
            dma((len(CHUNKS), 8)),
            dma((8,)),
            dma((8,)),
            dma((len(CHUNKS), others)),
            dma((len(CHUNKS), others)),
            dma((5, others)),
            dma((5, others)),
            dma((others,)),
            dma((others,)),
            dma((2 * RING - 1,)),
            dma((2 * RING - 1,)),
            *[pltpu.VMEM((RING, height, TILE), jnp.bfloat16) for height in CHUNKS],
            *[pltpu.VMEM(bundle, jnp.bfloat16)] * RING,
        ],
        compiler_params=pltpu.CompilerParams(
            collective_id=0, has_side_effects=True, vmem_limit_bytes=52 << 20
        ),
    )(index, matrix)


def solution(mesh):
    return jax.shard_map(
        on_device,
        mesh=mesh,
        in_specs=(P("wide", "narrow"), P(), P()),
        out_specs=P("wide", "narrow"),
        check_vma=False,
    )
```

```python
import jax
import jax.numpy as jnp
from jax import lax
from jax.experimental import pallas as pl
from jax.experimental.pallas import tpu as pltpu
from jax.sharding import PartitionSpec as P

TILE = 256
RING = 8
COLS = 8
FAN = 4
KEEP = 2
UPPER = 128
CHUNKS = (64, 64)
PIECE = 16
FAR_FIRST = (4, 3, 5, 2, 6, 1, 7)
MESH = pl.DeviceIdType.MESH


def place(step):
    step %= RING
    return 0 if step == 0 else 2 * step - 1 if step <= 4 else 2 * (RING - step)


def kernel(
    index_hbm,
    matrix,
    out,
    in_rows,
    cols,
    lower,
    outgoing,
    pieces,
    slots,
    panel,
    infl,
    result,
    sums,
    index_sem,
    load_sem,
    p_send,
    p_recv,
    y_send,
    y_recv,
    r_send,
    r_recv,
    z_send,
    z_recv,
    s_send,
    s_recv,
    x_send,
    x_recv,
    t_send,
    t_recv,
    *bundles,
):
    rings, planes = bundles[: len(CHUNKS)], bundles[len(CHUNKS) :]
    starts = [sum(CHUNKS[:c]) for c in range(len(CHUNKS))]
    row = lax.axis_index("wide")
    block = lax.axis_index("narrow")
    z = row // RING
    y = row % RING

    def along_y(step):
        return {"wide": z * RING + (y + step + RING) % RING}

    def along_z(step):
        return {"wide": ((z + step + RING) % RING) * RING + y}

    def along_x(step):
        return {"narrow": (block + step) % COLS}

    barrier = pltpu.get_barrier_semaphore()
    for step in range(1, RING):
        for target in (along_y(step), along_z(step), along_x(step)):
            pl.semaphore_signal(barrier, inc=1, device_id=target, device_id_type=MESH)
    index_load = pltpu.make_async_copy(index_hbm, in_rows, index_sem.at[0])
    index_load.start()
    loads = []
    for col in range(COLS):
        load = pltpu.make_async_copy(
            matrix.at[:, pl.ds(col * TILE, TILE)], cols.at[col], load_sem.at[col]
        )
        load.start()
        loads.append(load)
    index_load.wait()

    mine = jnp.int32(0)
    for col in range(COLS):
        for s in range(FAN):
            mine = jnp.where(in_rows[s, block * COLS + col] == row, col, mine)
    for load in loads:
        load.wait()
    own = cols[mine]
    panel[0] = own
    for ring, start, height in zip(rings, starts, CHUNKS):
        ring[0] = own[start : start + height]
    lower[...] = own[UPPER:].reshape(RING, PIECE, TILE)
    planes[0][0] = lower[y]
    pl.semaphore_wait(barrier, 3 * (RING - 1))

    started = []

    def send(src, dst, send_sem, recv_sem, target):
        copy = pltpu.make_async_remote_copy(
            src_ref=src,
            dst_ref=dst,
            send_sem=send_sem,
            recv_sem=recv_sem,
            device_id=target,
            device_id_type=MESH,
        )
        copy.start()
        started.append(copy)
        return copy

    def arrive(copies):
        for copy in copies:
            copy.wait_recv()

    parted = [
        send(
            lower.at[(y + d) % RING],
            planes[0].at[-d % RING],
            p_send.at[d - 1],
            p_recv.at[d - 1],
            along_y(d),
        )
        for d in FAR_FIRST
    ]
    def near(refs, send_sem, recv_sem, move):
        return [
            send(refs[0], refs[-d], send_sem.at[i], recv_sem.at[i], move(d))
            for i, d in enumerate((1, -1, 2, -2))
        ]

    def far(refs, distance, size, send_sem, recv_sem, move):
        copies = []
        for i, way in enumerate((1, -1)):
            part = pl.ds(0, size)
            if distance == 4:
                part = pl.ds(i * (size // 2), size // 2)
            copies.append(
                send(
                    refs[-way * (distance - 2)].at[part],
                    refs[-way * distance].at[part],
                    send_sem.at[2 * distance - 2 + i],
                    recv_sem.at[2 * distance - 2 + i],
                    move(2 * way),
                )
            )
        return copies

    z_sems = r_send, r_recv
    y_sems = [(y_send.at[c], y_recv.at[c]) for c in range(len(CHUNKS))]
    y_refs = [[ring.at[d] for d in range(RING)] for ring in rings]
    y_near = [near(y_refs[c], *y_sems[c], along_y) for c in range(len(CHUNKS))]
    gathers = [
        send(
            panel.at[0],
            panel.at[-d % COLS],
            x_send.at[d - 1],
            x_recv.at[d - 1],
            along_x(d),
        )
        for d in FAR_FIRST
    ]

    def holders(group, rows):
        found = [jnp.int32(0) for _ in rows]
        for k in range(RING):
            for t in range(FAN):
                named = in_rows[t, group * RING + k]
                for i, wanted in enumerate(rows):
                    found[i] = jnp.where(named == wanted, k, found[i])
        return [(k - y + RING) % RING for k in found]

    to_planes = holders(z, [((z + d) % RING) * RING + y for d in range(RING)])
    in_plane = [z * RING + (y + d) % RING for d in range(RING)]
    to_devices = {}
    for g in range(RING):
        to_devices[g] = holders((z + g) % RING, in_plane)

    across = []

    def hand_out(chunk):
        rows = pl.ds(starts[chunk], CHUNKS[chunk])
        for d in FAR_FIRST:
            outgoing[d, rows] = rings[chunk][to_planes[d]]
            across.append(
                send(
                    outgoing.at[d, rows],
                    slots.at[place(-d), rows],
                    z_send.at[chunk, d - 1],
                    z_recv.at[chunk, d - 1],
                    along_z(d),
                )
            )
        slots[0, rows] = rings[chunk][to_planes[0]]

    here = pl.ds(pl.multiple_of(UPPER + y * PIECE, PIECE), PIECE)

    def deal(distance):
        both = sorted({distance, -distance % RING})
        first = place(distance)
        group = pl.ds(first, len(both))
        for d in FAR_FIRST + (0,):
            for g in both:
                piece = planes[g][to_devices[g][d]]
                if d == 0:
                    slots[place(g), here] = piece
                else:
                    pieces[place(g), d] = piece
            if d:
                across.append(
                    send(
                        pieces.at[group, d],
                        slots.at[group, here],
                        s_send.at[distance, d - 1],
                        s_recv.at[distance, d - 1],
                        along_y(d),
                    )
                )

    y_far = {}

    def y_on(chunk):
        arrive(y_near[chunk])
        y_far[chunk] = [
            copy
            for distance in (3, 4)
            for copy in far(y_refs[chunk], distance, CHUNKS[chunk], *y_sems[chunk], along_y)
        ]

    arrive(parted)
    z_near = near(planes, *z_sems, along_z)
    y_on(0)
    arrive(z_near[:2])
    z_third = far(planes, 3, RING, *z_sems, along_z)
    y_on(1)
    arrive(z_near[2:])
    z_fourth = far(planes, 4, RING, *z_sems, along_z)
    deal(0)
    deal(1)
    arrive(y_far[0])
    hand_out(0)
    deal(2)
    arrive(z_third)
    deal(3)
    arrive(y_far[1])
    hand_out(1)
    arrive(z_fourth)
    deal(4)

    slots[RING] = jnp.zeros((TILE, TILE), jnp.bfloat16)
    lefts, rights, kept = [], [], []
    for col in range(COLS):
        column = block * COLS + col
        is_kept = jnp.bool_(False)
        for s in range(FAN):
            inner = in_rows[s, column]
            meets = jnp.bool_(False)
            for t in range(FAN):
                names = in_rows[t, inner] == row
                meets = meets | names
                if t < KEEP:
                    if s == 0 and t == 0:
                        is_kept = is_kept | names
                    else:
                        is_kept = is_kept | (names & (in_rows[FAN + s * KEEP + t, column] == 1))
            group = inner // RING
            lefts.append((group - block + COLS) % COLS)
            step = (group - z + RING) % RING
            slot = jnp.where(step <= 4, jnp.maximum(2 * step - 1, 0), 2 * (RING - step))
            rights.append(jnp.where(meets, slot, RING))
        kept.append(is_kept)

    arrive(gathers)
    arrive(across)

    for col in range(COLS):
        total = jnp.zeros((TILE, TILE), jnp.float32)
        for s in range(FAN):
            i = col * FAN + s
            total += jnp.dot(
                panel[lefts[i]], slots[rights[i]], preferred_element_type=jnp.float32
            )
        total = jnp.where(kept[col], total, jnp.float32(0.0))
        square = total * total
        infl[col] = square
        sums[0, pl.ds(col, 1)] = jnp.sum(square, axis=0, keepdims=True)

    def add_up(first, move, earlier):
        copies = [
            send(
                sums.at[first],
                sums.at[first + d],
                t_send.at[first + d - 1],
                t_recv.at[first + d - 1],
                move(d),
            )
            for d in FAR_FIRST
        ]
        for copy in earlier:
            copy.wait_send()
        arrive(copies)
        total = sums[first]
        for d in range(1, RING):
            total += sums[first + d]
        return total

    sums[RING] = add_up(0, along_y, started[:])
    last = started[-(RING - 1) :]
    scale = jnp.float32(TILE) / add_up(RING, along_z, last)
    stores = []
    for col in range(COLS):
        result[col] = (infl[col] * scale[col : col + 1]).astype(jnp.bfloat16)
        store = pltpu.make_async_copy(
            result.at[col], out.at[:, pl.ds(col * TILE, TILE)], load_sem.at[col]
        )
        store.start()
        stores.append(store)
    for copy in started[-(RING - 1) :]:
        copy.wait_send()
    for store in stores:
        store.wait()


def on_device(matrix, in_rows, keep):
    index = jnp.concatenate([in_rows, keep.reshape(-1, FAN * KEEP)], axis=1).T
    tile = (TILE, TILE)
    bundle = (RING, PIECE, TILE)
    dma = pltpu.SemaphoreType.DMA
    others = RING - 1
    hbm = pl.BlockSpec(memory_space=pltpu.HBM)
    return pl.pallas_call(
        kernel,
        out_shape=jax.ShapeDtypeStruct(matrix.shape, jnp.bfloat16),
        in_specs=[hbm, hbm],
        out_specs=hbm,
        scratch_shapes=[
            pltpu.SMEM(index.shape, jnp.int32),
            pltpu.VMEM((COLS, *tile), jnp.bfloat16),
            pltpu.VMEM(bundle, jnp.bfloat16),
            pltpu.VMEM((RING, UPPER, TILE), jnp.bfloat16),
            pltpu.VMEM((RING, *bundle), jnp.bfloat16),
            pltpu.VMEM((RING + 1, *tile), jnp.bfloat16),
            pltpu.VMEM((COLS, *tile), jnp.bfloat16),
            pltpu.VMEM((COLS, *tile), jnp.float32),
            pltpu.VMEM((COLS, *tile), jnp.bfloat16),
            pltpu.VMEM((2 * RING, COLS, TILE), jnp.float32),
            dma((1,)),
            dma((COLS,)),
            dma((others,)),
            dma((others,)),
            dma((len(CHUNKS), 8)),
            dma((len(CHUNKS), 8)),
            dma((8,)),
            dma((8,)),
            dma((len(CHUNKS), others)),
            dma((len(CHUNKS), others)),
            dma((5, others)),
            dma((5, others)),
            dma((others,)),
            dma((others,)),
            dma((2 * RING - 1,)),
            dma((2 * RING - 1,)),
            *[pltpu.VMEM((RING, height, TILE), jnp.bfloat16) for height in CHUNKS],
            *[pltpu.VMEM(bundle, jnp.bfloat16)] * RING,
        ],
        compiler_params=pltpu.CompilerParams(
            collective_id=0, has_side_effects=True, vmem_limit_bytes=52 << 20
        ),
    )(index, matrix)


def solution(mesh):
    return jax.shard_map(
        on_device,
        mesh=mesh,
        in_specs=(P("wide", "narrow"), P(), P()),
        out_specs=P("wide", "narrow"),
        check_vma=False,
    )
```
